32 devices in a mesh: dp: 2 (over core), head: 2 (over x), ctx: 8 (over z, y).
Axes of the slice: x: 2, y: 2, z: 4, core: 2. Of those that a mesh axis runs over, the one named last changes fastest.
Arguments:
- query_states: bfloat16 [2, 8192, 32, 128], P('dp', 'ctx', 'head'), may hold values from -6 to 6
- key_states: bfloat16 [2, 8192, 8, 128], P('dp', 'ctx', 'head'), may hold values from -6 to 6
- value_states: bfloat16 [2, 8192, 8, 128], P('dp', 'ctx', 'head'), may hold values from -12 to 12
- gate_values: float32 [32], P('head'), may hold values from 0.1 to 0.9
- head_flags: int32 [32], P('head'), may hold values from 0 to 1, as said below
- output_grad: bfloat16 [2, 8192, 32, 128], P('dp', 'ctx', 'head'), may hold values from -16 to 16
Outputs:
- blended: bfloat16 [2, 8192, 32, 128], P('dp', 'ctx', 'head')
- gate_grad: float32 [32], replicated
The draws below stay inside these ranges and needn't reach their ends.
Inputs may be any that keep to these rules, and one draw needn't show every extreme that they name: `head_flags`: exactly 1 of the 4 query heads of each key-value head have flag 1.
All inputs are finite; a program needn't handle non-finite values.
Results may differ from the reference program's by a relative error of at most 0.005.
Values may be sent and summed in bfloat16 or wider, within the bound.
A program may use at most 128 MiB of HBM per device.

```python
import math
import jax
import jax.numpy as jnp
from jax import lax

HD = 128
KVH = 8
QPG = 4
RET = 1
SINK = 64
WINDOW = 2048
SEQS = 2
L = 8192
H = 32


def draw_query_states(seed_key, part_index):
    own_key = jax.random.fold_in(seed_key, 11)
    drawn = 1.5 * jax.random.normal(jax.random.fold_in(own_key, 3), (SEQS, L, H, HD), jnp.float32)
    return jnp.clip(drawn, -6.0, 6.0).astype(jnp.bfloat16)


def draw_key_states(seed_key, part_index):
    own_key = jax.random.fold_in(seed_key, 21)
    sink_scale = jnp.where(jnp.arange(L) < SINK, 1.8, 1.0).astype(jnp.float32)[None, :, None, None]
    drawn = jax.random.normal(jax.random.fold_in(own_key, 2), (SEQS, L, KVH, HD), jnp.float32) * sink_scale
    return jnp.clip(drawn, -6.0, 6.0).astype(jnp.bfloat16)


def draw_output_grad(seed_key, part_index):
    own_key = jax.random.fold_in(seed_key, 31)
    fraction = (jnp.arange(L, dtype=jnp.float32) / (L - 1))[None, :, None, None]
    ramp_scale = jnp.exp(fraction * math.log(3.0))
    drawn = jnp.clip(jax.random.normal(jax.random.fold_in(own_key, 3), (SEQS, L, H, HD), jnp.float32), -5.0, 5.0) * ramp_scale
    return drawn.astype(jnp.bfloat16)


def pick_order(split_key):
    return jax.random.permutation(split_key, QPG)


def draw_head_flags(seed_key, part_index):
    split_keys = jax.random.split(jax.random.fold_in(seed_key, 41), KVH)
    orders = jax.vmap(pick_order)(split_keys)
    return (orders < RET).astype(jnp.int32).reshape(H)


def shard_levels(rng, shape, cuts, least, top_value):
    def one(dim, blocks):
        heights = jax.random.uniform(jax.random.fold_in(jax.random.fold_in(rng, 6), dim), (blocks,), jnp.float32, least / len(cuts), top_value / len(cuts))
        return jnp.repeat(jnp.exp(heights), shape[dim] // blocks).reshape((-1,) + (1,) * (len(shape) - dim - 1))

    gain = one(*cuts[0])
    for cut in cuts[1:]:
        gain = gain * one(*cut)
    return gain


def gaussian(key, dims, scale, limit, cuts=(), held_as=jnp.bfloat16):
    values = scale * jax.random.normal(key, dims, jnp.float32)
    if cuts:
        values = values * shard_levels(key, dims, cuts, -0.22, 0.18)
    return jnp.clip(values, -limit, limit).astype(held_as)


def setup_inputs(seed: int = 0) -> dict:
    key_of = jax.random.split(jax.random.key(seed), 7)
    return {
        "query_states": draw_query_states(jax.random.fold_in(key_of[6], 71), 0),
        "key_states": draw_key_states(jax.random.fold_in(key_of[6], 71), 0),
        "value_states": gaussian(key_of[2], (SEQS, L, KVH, HD), 2.0, 12.0, ((0, 2), (1, 8), (2, 2))),
        "gate_values": jnp.clip(0.1 + 0.79999997 * jax.random.uniform(key_of[3], (H,), jnp.float32) ** shard_levels(key_of[3], (H,), ((0, 2),), -0.2, 0.2), 0.1, 0.9),
        "head_flags": draw_head_flags(jax.random.fold_in(key_of[6], 71), 0),
        "output_grad": draw_output_grad(jax.random.fold_in(key_of[6], 71), 0),
    }


def weighted_mix(query_block, key_rows, value_rows, allowed):
    scores = jnp.einsum('rgeh,kgh->rgek', query_block.astype(jnp.float32), key_rows.astype(jnp.float32)) * (1.0 / math.sqrt(HD))
    visible = allowed[:, None, None, :]
    scores = jnp.where(visible, scores, -jnp.inf)
    highest = lax.optimization_barrier(jnp.max(scores, axis=-1, keepdims=True))
    weights = jnp.where(visible, jnp.exp(scores - highest), 0.0)
    denominator = lax.optimization_barrier(jnp.sum(weights, axis=-1))
    rounded = lax.optimization_barrier(weights.astype(jnp.bfloat16)).astype(jnp.float32)
    numerator = jnp.einsum('rgek,kgh->rgeh', rounded, value_rows.astype(jnp.float32))
    return numerator / denominator[..., None]

def one_sequence(picker, query_seq, key_seq, value_seq):
    row_block = math.gcd(L, 512)
    positions = jnp.arange(L, dtype=jnp.int32)
    chosen = jnp.einsum('gre,lgeh->lgrh', picker, query_seq.astype(jnp.float32), precision=lax.Precision.HIGHEST)
    starts = jnp.arange(L // row_block, dtype=jnp.int32) * row_block

    def full_block(first_row):
        row_pos = first_row + jnp.arange(row_block, dtype=jnp.int32)
        query_block = lax.dynamic_slice_in_dim(chosen, first_row, row_block)
        return weighted_mix(query_block, key_seq, value_seq, positions[None, :] <= row_pos[:, None])
    full_ret = lax.map(full_block, starts).reshape(L, KVH, RET, HD)
    full_all = jnp.einsum('gre,lgrh->lgeh', picker, full_ret, precision=lax.Precision.HIGHEST)
    pad_keys = jnp.concatenate([jnp.zeros((WINDOW, KVH, HD), key_seq.dtype), key_seq], axis=0)
    pad_values = jnp.concatenate([jnp.zeros((WINDOW, KVH, HD), value_seq.dtype), value_seq], axis=0)
    sink_pos = jnp.arange(SINK, dtype=jnp.int32)

    def near_block(first_row):
        row_pos = first_row + jnp.arange(row_block, dtype=jnp.int32)
        query_block = lax.dynamic_slice_in_dim(query_seq, first_row, row_block)
        near_pos = first_row - WINDOW + jnp.arange(WINDOW + row_block, dtype=jnp.int32)
        near_ok = (near_pos[None, :] >= 0) & (near_pos[None, :] <= row_pos[:, None]) & (row_pos[:, None] - near_pos[None, :] < WINDOW)
        sink_ok = (sink_pos[None, :] <= row_pos[:, None]) & (row_pos[:, None] - sink_pos[None, :] >= WINDOW)
        key_rows = jnp.concatenate([key_seq[:SINK], lax.dynamic_slice_in_dim(pad_keys, first_row, WINDOW + row_block)], axis=0)
        value_rows = jnp.concatenate([value_seq[:SINK], lax.dynamic_slice_in_dim(pad_values, first_row, WINDOW + row_block)], axis=0)
        return weighted_mix(query_block, key_rows, value_rows, jnp.concatenate([sink_ok, near_ok], axis=1))
    near_all = lax.map(near_block, starts).reshape(L, KVH, QPG, HD)
    return (full_all, near_all)

def reference(query_states, key_states, value_states, gate_values, head_flags, output_grad):
    marked = head_flags.reshape(KVH, QPG)
    ordinal = jnp.cumsum(marked, axis=1) - 1
    slot_ids = jnp.arange(RET, dtype=jnp.int32)
    picker = ((marked[:, None, :] == 1) & (ordinal[:, None, :] == slot_ids[None, :, None])).astype(jnp.float32)
    queries = query_states.reshape(SEQS, L, KVH, QPG, HD)

    def per_sequence(members):
        return one_sequence(picker, members[0], members[1], members[2])
    full_all, near_all = lax.map(per_sequence, (queries, key_states, value_states))
    gate_cols = gate_values.reshape(KVH, QPG)[:, :, None]
    retrieval = (marked == 1)[:, :, None]
    mixed = jnp.where(retrieval, gate_cols * full_all + (1.0 - gate_cols) * near_all, near_all)
    blended = mixed.astype(jnp.bfloat16).reshape(SEQS, L, H, HD)
    grad_rows = output_grad.reshape(SEQS, L, KVH, QPG, HD).astype(jnp.float32)
    gate_terms = lax.optimization_barrier(jnp.sum(grad_rows * (full_all - near_all), axis=(0, 1, 4))) * marked.astype(jnp.float32)
    gate_grad = gate_terms.reshape(H) * (1.0 / math.sqrt(SEQS * L * HD))
    return (blended, gate_grad)
```

```python
import functools
import math

import jax
import jax.numpy as jnp
from jax import lax
from jax.experimental import pallas as pl
from jax.experimental.pallas import tpu as pltpu
from jax.sharding import PartitionSpec as P

SINK = 64
WINDOW = 2048
BLOCK = 512
LANES = 128
NT = (((1,), (1,)), ((), ()))


def lane_sum(weights):
    total = weights[:, :LANES]
    for at in range(LANES, weights.shape[1], LANES):
        total = total + weights[:, at : at + LANES]
    return total


def update(m_ref, l_ref, acc_ref, query, keys, values, factor, mask, first=False):
    scores = lax.dot_general(query, keys, NT, preferred_element_type=jnp.float32)
    if mask is not None:
        scores = jnp.where(mask, scores, -jnp.inf)
    highest = jnp.max(scores, axis=1, keepdims=True)
    if not first:
        before = m_ref[:, :1]
        highest = jnp.maximum(before, highest)
    weights = jnp.exp2((scores - highest) * factor)
    part = jnp.dot(weights.astype(jnp.bfloat16), values, preferred_element_type=jnp.float32)
    sums = lane_sum(weights)
    if first:
        l_ref[...] = sums
        acc_ref[...] = part
    else:
        shrink = jnp.exp2((before - highest) * factor)
        l_ref[...] = l_ref[...] * shrink + sums
        acc_ref[...] = acc_ref[...] * shrink + part
    m_ref[...] = jnp.broadcast_to(highest, m_ref.shape)


def grid_of(rows, cols):
    shape = (rows, cols)
    return lax.broadcasted_iota(jnp.int32, shape, 0), lax.broadcasted_iota(jnp.int32, shape, 1)


def near_kernel(per_group, factor, meta, q, k, v, sk, sv, out, om, ol, oacc, m, l, acc):
    group, qb = pl.program_id(0), pl.program_id(1)
    back = WINDOW // BLOCK
    first_row = meta[0] + qb * BLOCK
    heads = range(per_group)

    def visit(block, mask, first=False):
        rows = pl.ds(pl.multiple_of(block * BLOCK, BLOCK), BLOCK)
        keys, values = k[rows, :], v[rows, :]
        for e in heads:
            query = q[:, e * LANES : (e + 1) * LANES]
            update(m.at[e], l.at[e], acc.at[e], query, keys, values, factor, mask, first)

    row, col = grid_of(BLOCK, BLOCK)
    visit(qb + back, col <= row, True)

    def middle(block, _):
        visit(block, None)
        return 0

    valid_from = back - meta[0] // BLOCK
    lax.fori_loop(jnp.maximum(qb + 1, valid_from), qb + back, middle, 0)

    @pl.when(first_row >= WINDOW)
    def _():
        row2, col2 = grid_of(BLOCK, BLOCK)
        visit(qb, col2 > row2)
        srow, scol = grid_of(BLOCK, LANES)
        seen = (scol < SINK) & (scol <= srow + first_row - WINDOW)
        for e in heads:
            query = q[:, e * LANES : (e + 1) * LANES]
            update(m.at[e], l.at[e], acc.at[e], query, sk[...], sv[...], factor, seen)

    for e in heads:
        total = jnp.sum(l[e], axis=1, keepdims=True)
        out[:, e * LANES : (e + 1) * LANES] = (acc[e] / total).astype(jnp.bfloat16)

    slot = meta[1 + group]
    om[0] = m[slot]
    ol[0] = l[slot]
    oacc[0] = acc[slot]


def far_kernel(groups, factor, meta, gates, q, k, v, og, m0, l0, a0, base, out, grad, m, l, acc):
    del base
    group, qb = pl.program_id(0), pl.program_id(1)
    first_row = meta[0] + qb * BLOCK
    m[...] = m0[0]
    l[...] = l0[0]
    acc[...] = a0[0]

    def visit(block, mask):
        rows = pl.ds(pl.multiple_of(block * BLOCK, BLOCK), BLOCK)
        update(m, l, acc, q[...], k[rows, :], v[rows, :], factor, mask)

    last = (first_row - WINDOW) // BLOCK

    @pl.when(first_row >= WINDOW)
    def _():
        row, col = grid_of(BLOCK, BLOCK)
        visit(last, (col <= row) & (col + last * BLOCK >= SINK))

    @pl.when(first_row > WINDOW)
    def _():
        _, col = grid_of(BLOCK, BLOCK)
        visit(0, col >= SINK)

    def middle(block, _):
        visit(block, None)
        return 0

    lax.fori_loop(1, last, middle, 0)
    near = a0[0] / jnp.sum(l0[0], axis=1, keepdims=True)
    full = acc[...] / jnp.sum(l[...], axis=1, keepdims=True)
    gate = gates[group]
    out[...] = (gate * full + (1.0 - gate) * near).astype(jnp.bfloat16)
    terms = og[...].astype(jnp.float32) * (full - near)
    grad[0, 0] = jnp.sum(terms.reshape(BLOCK // 8, 8, LANES), axis=0)


def from_behind(block, axis, distance):
    devices = range(lax.axis_size(axis))
    route = [(i - distance, i) for i in devices if i - distance in devices]
    return lax.ppermute(block, axis, route)


def on_device(query_states, key_states, value_states, gate_values, head_flags, output_grad):
    tok = query_states.shape[1]
    groups, width = key_states.shape[2], key_states.shape[3]
    heads = query_states.shape[2]
    per = heads // groups
    ctx_count = lax.axis_size("ctx")
    seq = tok * ctx_count
    depth = WINDOW // tok
    factor = math.log2(math.e) / math.sqrt(width)
    queries = query_states.reshape(tok, heads * width)
    grads = output_grad.reshape(tok, heads * width)
    kv = jnp.concatenate(
        [key_states.reshape(tok, groups * width), value_states.reshape(tok, groups * width)], axis=1
    )
    earlier = [from_behind(kv, "ctx", d) for d in range(depth, 0, -1)]
    near_kv = jnp.concatenate(earlier + [kv], axis=0)
    sinks = lax.all_gather(kv[:SINK], "ctx", axis=0)[0]
    sinks = jnp.pad(sinks, ((0, LANES - SINK), (0, 0)))
    all_kv = lax.all_gather(kv, "ctx", axis=0, tiled=True)

    marked = head_flags.reshape(groups, per)
    slots = jnp.argmax(marked, axis=1).astype(jnp.int32)
    start = (lax.axis_index("ctx") * tok).astype(jnp.int32)
    meta = jnp.concatenate([start[None], slots])
    gates = jnp.sum(gate_values.reshape(groups, per) * marked.astype(jnp.float32), axis=1)
    qblocks = tok // BLOCK
    grid = (groups, qblocks)
    state = jax.ShapeDtypeStruct((groups, tok, LANES), jnp.float32)
    state_spec = pl.BlockSpec((1, BLOCK, LANES), lambda g, i, *_: (g, i, 0))
    span = near_kv.shape[0]
    params = pltpu.CompilerParams(vmem_limit_bytes=40 * 1024 * 1024)

    near_pairs = heads * tok * (WINDOW + BLOCK)
    near_out, m0, l0, a0 = pl.pallas_call(
        functools.partial(near_kernel, per, factor),
        grid_spec=pltpu.PrefetchScalarGridSpec(
            num_scalar_prefetch=1,
            grid=grid,
            in_specs=[
                pl.BlockSpec((BLOCK, per * width), lambda g, i, *_: (i, g)),
                pl.BlockSpec((span, width), lambda g, i, *_: (0, g)),
                pl.BlockSpec((span, width), lambda g, i, *_: (0, groups + g)),
                pl.BlockSpec((LANES, width), lambda g, i, *_: (0, g)),
                pl.BlockSpec((LANES, width), lambda g, i, *_: (0, groups + g)),
            ],
            out_specs=[
                pl.BlockSpec((BLOCK, per * width), lambda g, i, *_: (i, g)),
                state_spec,
                state_spec,
                state_spec,
            ],
            scratch_shapes=[pltpu.VMEM((per, BLOCK, LANES), jnp.float32)] * 3,
        ),
        out_shape=[jax.ShapeDtypeStruct((tok, heads * width), jnp.bfloat16), state, state, state],
        compiler_params=params,
        cost_estimate=pl.CostEstimate(
            flops=4 * near_pairs * width, bytes_accessed=32 << 20, transcendentals=near_pairs
        ),
        name="near",
    )(meta, queries, near_kv, near_kv, sinks, sinks)

    far_pairs = groups * tok * seq
    mine = pl.BlockSpec((BLOCK, width), lambda g, i, meta, *_: (i, g * per + meta[1 + g]))
    blended, partial = pl.pallas_call(
        functools.partial(far_kernel, groups, factor),
        grid_spec=pltpu.PrefetchScalarGridSpec(
            num_scalar_prefetch=2,
            grid=grid,
            in_specs=[
                mine,
                pl.BlockSpec((seq, width), lambda g, i, *_: (0, g)),
                pl.BlockSpec((seq, width), lambda g, i, *_: (0, groups + g)),
                mine,
                state_spec,
                state_spec,
                state_spec,
                pl.BlockSpec(memory_space=pl.ANY),
            ],
            out_specs=[
                mine,
                pl.BlockSpec((1, 1, 8, LANES), lambda g, i, *_: (g, i, 0, 0)),
            ],
            scratch_shapes=[pltpu.VMEM((BLOCK, LANES), jnp.float32)] * 3,
        ),
        out_shape=[
            jax.ShapeDtypeStruct((tok, heads * width), jnp.bfloat16),
            jax.ShapeDtypeStruct((groups, qblocks, 8, LANES), jnp.float32),
        ],
        input_output_aliases={9: 0},
        compiler_params=params,
        cost_estimate=pl.CostEstimate(
            flops=2 * far_pairs * width, bytes_accessed=32 << 20, transcendentals=far_pairs // 2
        ),
        name="far",
    )(meta, gates, queries, all_kv, all_kv, grads, m0, l0, a0, near_out)

    local = (jnp.sum(partial, axis=(1, 2, 3))[:, None] * marked.astype(jnp.float32)).reshape(heads)
    padded = lax.dynamic_update_slice_in_dim(
        jnp.zeros((heads * lax.axis_size("head"),), jnp.float32),
        local,
        lax.axis_index("head") * heads,
        0,
    )
    totals = lax.psum(padded, ("dp", "head", "ctx"))
    count = lax.axis_size("dp") * query_states.shape[0] * seq * width
    return blended.reshape(1, tok, heads, width), totals * (1.0 / math.sqrt(count))


def solution(mesh):
    return jax.shard_map(
        on_device,
        mesh=mesh,
        in_specs=(
            P("dp", "ctx", "head", None),
            P("dp", "ctx", "head", None),
            P("dp", "ctx", "head", None),
            P("head"),
            P("head"),
            P("dp", "ctx", "head", None),
        ),
        out_specs=(P("dp", "ctx", "head", None), P()),
        check_vma=False,
    )
```
